32 devices in a mesh: rep: 8 (over z, y), tp: 4 (over x, core).
Axes of the slice: x: 2, y: 2, z: 4, core: 2. Of those that a mesh axis runs over, the one named last changes fastest.
Arguments:
- hidden: bfloat16 [8192, 2560], P(('rep', 'tp')), may hold values from -6 to 6
- cotangent: bfloat16 [8192, 512], P('rep', 'tp'), may hold values from -6 to 6
- numerator: float32 [8, 2560, 512], P('rep', None, 'tp'), may hold values from -0.125 to 0.125
- push_weight: float32 [8], P('rep'), as said below
- moment_one: float32 [8, 2560, 512], P('rep', None, 'tp'), may hold values from -180 to 180
- moment_two: float32 [8, 2560, 512], P('rep', None, 'tp'), may hold values from 100 to 10000
- gossip_round: int32 [3], replicated, may hold values from 0 to 2, as said below
Outputs:
- numerator_out: float32 [8, 2560, 512], P('rep', None, 'tp')
- weight_out: float32 [8], P('rep')
- moment_one_out: float32 [8, 2560, 512], P('rep', None, 'tp')
- moment_two_out: float32 [8, 2560, 512], P('rep', None, 'tp')
- values: bfloat16 [8192, 512], P('rep', 'tp')
- grad_hidden: bfloat16 [8192, 2560], P(('rep', 'tp'))
The draws below stay inside these ranges and needn't reach their ends.
Inputs may be any that keep to these rules, and one draw needn't show every extreme that they name: `gossip_round`: each of the rounds 0, 1, 2 once. `push_weight`: positive.
All inputs are finite; a program needn't handle non-finite values.
Results may differ from the reference program's by a relative error of at most 0.015.
Values may be sent and summed in bfloat16 or wider, within the bound.
A program may use at most 64 MiB of HBM per device.

```python
import math
import jax
import jax.numpy as jnp
from jax import lax

DW = 2560
KV = 512
TOK_DEV = 1024
TOKENS = 8192
N_REP = 8
N_TP = 4


def draw_push_weight(key, part):
    key = jax.random.fold_in(key, 11)
    expo = jax.random.uniform(key, (N_REP,), jnp.float32, -1.0, 1.0)
    return jnp.exp2(expo).astype(jnp.float32)


def draw_gossip_round(key, part):
    key = jax.random.fold_in(key, 23)
    return jax.random.permutation(key, jnp.arange(3, dtype=jnp.int32)).astype(jnp.int32)


def levels(stream_key, dims, shards, smallest, top_value):
    loudness = 1.0
    for dim, parts in shards:
        draws = jax.random.uniform(jax.random.fold_in(jax.random.fold_in(stream_key, 6), dim), (parts,), jnp.float32, smallest / len(shards), top_value / len(shards))
        loudness = loudness * jnp.repeat(jnp.exp(draws), dims[dim] // parts).reshape((-1,) + (1,) * (len(dims) - 1 - dim))
    return loudness


def scatter_about(own_key, extent, spread, bound, shards=(), held_as=jnp.bfloat16):
    factor_of = levels(own_key, extent, shards, -0.22, 0.18) if shards else 1.0
    values = jax.random.normal(own_key, extent, jnp.float32) * spread * factor_of
    return jnp.minimum(jnp.maximum(values, -bound), bound).astype(held_as)


def setup_inputs(seed: int = 0) -> dict:
    splits = jax.random.split(jax.random.key(seed), 8)
    hidden = scatter_about(splits[0], (TOKENS, DW), 1.0, 6.0, ((0, 32),))
    cotangent = scatter_about(splits[1], (TOKENS, KV), 1.0, 6.0, ((0, 8), (1, 4)))
    numerator = scatter_about(splits[2], (N_REP, DW, KV), DW ** -0.5, 0.125, ((0, 8), (2, 4)), jnp.float32)
    push_weight = draw_push_weight(jax.random.fold_in(splits[7], 71), 0)
    moment_one = scatter_about(splits[4], (N_REP, DW, KV), 30.0, 180.0, ((0, 8), (2, 4)), jnp.float32)
    moment_two = jnp.clip(jnp.exp(math.log(10000.0) - 4.6051702 * jax.random.uniform(splits[5], (N_REP, DW, KV), jnp.float32) ** levels(splits[5], (N_REP, DW, KV), ((0, 8), (2, 4)), -0.2, 0.2)), 100.0, 10000.0)
    gossip_round = draw_gossip_round(jax.random.fold_in(splits[7], 71), 0)
    return {"hidden": hidden, "cotangent": cotangent, "numerator": numerator, "push_weight": push_weight, "moment_one": moment_one, "moment_two": moment_two, "gossip_round": gossip_round}


def one_replica(items):
    hidden, cotangent, numerator, weight, moment_one, moment_two = items
    hid = hidden.astype(jnp.float32)
    scale = lax.rsqrt(lax.optimization_barrier(jnp.mean(hid * hid, axis=1, keepdims=True)) + 1e-06)
    normal = hid * scale
    normed = normal.astype(jnp.bfloat16)
    plain = numerator / weight
    debiased = plain.astype(jnp.bfloat16)
    values = jnp.dot(normed, debiased, preferred_element_type=jnp.float32).astype(jnp.bfloat16)
    grad = lax.dot_general(normed, cotangent, (((0,), (0,)), ((), ())), preferred_element_type=jnp.float32)
    block = KV // N_TP
    grad_normed = jnp.zeros(hid.shape, jnp.float32)
    for index in range(N_TP):
        cot_cols = cotangent[:, index * block:(index + 1) * block]
        deb_cols = debiased[:, index * block:(index + 1) * block]
        term = lax.dot_general(cot_cols, deb_cols, (((1,), (1,)), ((), ())), preferred_element_type=jnp.float32)
        term = lax.optimization_barrier(term.astype(jnp.bfloat16))
        grad_normed = grad_normed + term.astype(jnp.float32)
    inner = lax.optimization_barrier(jnp.mean(grad_normed * normal, axis=1, keepdims=True))
    grad_hidden = (scale * (grad_normed - normal * inner)).astype(jnp.bfloat16)
    first = 0.9 * moment_one + 0.1 * grad
    second = 0.95 * moment_two + 0.05 * grad * grad
    half = numerator - 0.001 * (first / (jnp.sqrt(second) + 1e-08) + 0.1 * plain)
    return (half, first, second, values, grad_hidden)

def reference(hidden, cotangent, numerator, push_weight, moment_one, moment_two, gossip_round):
    hid_all = hidden.reshape(N_REP, TOK_DEV, DW)
    cot_all = cotangent.reshape(N_REP, TOK_DEV, KV)
    half, first, second, values, grad_hidden = lax.map(one_replica, (hid_all, cot_all, numerator, push_weight, moment_one, moment_two))
    distance = jnp.left_shift(jnp.int32(1), gossip_round[0].astype(jnp.int32))
    numerator_out = 0.5 * (half + jnp.roll(half, distance, axis=0))
    weight_out = 0.5 * (push_weight + jnp.roll(push_weight, distance, axis=0))
    return (numerator_out, weight_out, first, second, values.reshape(TOKENS, KV), grad_hidden.reshape(TOKENS, DW))
```

```python
import functools

import jax
import jax.numpy as jnp
from jax import lax
from jax.experimental import pallas as pl
from jax.experimental.pallas import tpu as pltpu
from jax.sharding import PartitionSpec as P

MESH = pl.DeviceIdType.MESH
F32 = jnp.float32
BF16 = jnp.bfloat16
ROUNDS = 3
CHUNKS = 5
EARLY = 1


def kernel(
    dist, chunks,
    w_ref, hid_hbm, cot_hbm, num_hbm, m1_hbm, m2_hbm,
    numo_hbm, wo_ref, m1o_hbm, m2o_hbm, val_hbm, gh_hbm,
    hid, num, m1, m2, cot_own, cot_far, nrm, scale,
    deb_own, deb_far, g_own, g_send, g_far, half, half_send, half_far,
    gn, gn_send, gn_near, gh, val_acc, val_own, val_send, w_send, w_far,
    load_sem, write_sem,
    cot_s, cot_r, nrm_s, nrm_r, deb_s, deb_r, g_s, g_r, half_s, half_r, gn_s, gn_r, val_s, val_r, w_s, w_r,
):
    rows, width = hid.shape
    fc = width // chunks
    rep, tp = lax.axis_index("rep"), lax.axis_index("tp")
    n_rep = lax.axis_size("rep")
    near = tp + 1 - 2 * lax.rem(tp, 2)
    far = lax.rem(tp + 2, 4)
    far_near = lax.rem(near + 2, 4)
    to_rep = lax.rem(rep + dist, n_rep)
    from_rep = lax.rem(rep + n_rep - dist, n_rep)
    near_dev, far_dev, to_dev, from_dev = (rep, near), (rep, far), (to_rep, tp), (from_rep, tp)

    def row_block(index):
        return pl.ds(pl.multiple_of(index * rows, rows), rows)

    loads = [
        pltpu.make_async_copy(hid_hbm, hid, load_sem.at[0]),
        pltpu.make_async_copy(num_hbm.at[0], num, load_sem.at[1]),
        pltpu.make_async_copy(cot_hbm.at[row_block(tp)], cot_own.at[pl.ds(0, rows)], load_sem.at[2]),
        pltpu.make_async_copy(cot_hbm.at[row_block(near)], cot_own.at[pl.ds(rows, rows)], load_sem.at[3]),
        pltpu.make_async_copy(m1_hbm.at[0], m1, load_sem.at[4]),
        pltpu.make_async_copy(m2_hbm.at[0], m2, load_sem.at[5]),
    ]
    for load in loads:
        load.start()

    barrier = pltpu.get_barrier_semaphore()
    for device in (near_dev, far_dev, to_dev, from_dev):
        pl.semaphore_signal(barrier, inc=1, device_id=device, device_id_type=MESH)
    pl.semaphore_wait(barrier, 4)

    def remote(src, dst, send, recv, device):
        return pltpu.make_async_remote_copy(
            src_ref=src, dst_ref=dst, send_sem=send, recv_sem=recv, device_id=device, device_id_type=MESH
        )

    cot_copies = [
        remote(cot_hbm.at[row_block(far)], cot_far.at[pl.ds(0, rows)], cot_s.at[0], cot_r.at[0], far_dev),
        remote(cot_hbm.at[row_block(far_near)], cot_far.at[pl.ds(rows, rows)], cot_s.at[1], cot_r.at[1], far_dev),
    ]
    for copy in cot_copies:
        copy.start()
    part = [pl.ds(c * fc, fc) for c in range(chunks)]
    nrm_copies = [
        remote(nrm.at[c, pl.ds(0, rows)], nrm.at[c, pl.ds(rows, rows)], nrm_s.at[c], nrm_r.at[c], near_dev)
        for c in range(chunks)
    ]
    deb_copies = [
        remote(deb_own.at[part[c]], deb_far.at[part[c]], deb_s.at[c], deb_r.at[c], far_dev) for c in range(chunks)
    ]
    g_copies = [
        remote(g_send.at[part[c]], g_far.at[part[c]], g_s.at[c], g_r.at[c], far_dev) for c in range(chunks)
    ]
    half_copies = [
        remote(half_send.at[part[c]], half_far.at[part[c]], half_s.at[c], half_r.at[c], to_dev)
        for c in range(chunks)
    ]
    gn_copies = [
        remote(gn_send.at[c], gn_near.at[c], gn_s.at[c], gn_r.at[c], near_dev) for c in range(chunks)
    ]
    val_copies = [
        remote(val_send.at[pl.ds(0, rows)], val_hbm.at[row_block(tp)], val_s.at[0], val_r.at[0], far_dev),
        remote(val_send.at[pl.ds(rows, rows)], val_hbm.at[row_block(near)], val_s.at[1], val_r.at[1], far_dev),
    ]
    weight = w_ref[0]
    w_send[...] = jnp.full(w_send.shape, weight, F32)
    w_copy = remote(w_send, w_far, w_s.at[0], w_r.at[0], to_dev)
    w_copy.start()

    loads[0].wait()
    step = 32

    @pl.loop(0, rows // step)
    def _(block):
        here = pl.ds(pl.multiple_of(block * step, step), step)
        x = hid[here, :].astype(F32)
        s = lax.rsqrt(jnp.mean(x * x, axis=1, keepdims=True) + 1e-06)
        scale[here, :] = s
        y = (x * s).astype(BF16)
        for c in range(chunks):
            nrm[c, here, :] = y[:, c * fc:(c + 1) * fc]

    for copy in nrm_copies:
        copy.start()

    loads[1].wait()

    def send_deb(c):
        deb_own[part[c], :] = (num[part[c], :] / jnp.full((1, 1), weight, F32)).astype(BF16)
        deb_copies[c].start()

    for c in range(EARLY):
        send_deb(c)

    loads[2].wait()
    loads[3].wait()
    for copy in cot_copies:
        copy.wait_recv()
    cot2 = jnp.concatenate([cot_own[...], cot_far[...]], axis=1)
    k = cot_own.shape[1]
    for c in range(chunks):
        nrm_copies[c].wait_recv()
        p = lax.dot_general(nrm[c], cot2, (((0,), (0,)), ((), ())), preferred_element_type=F32)
        g_send[part[c], :] = p[:, k:].astype(BF16)
        g_copies[c].start()
        g_own[part[c], :] = p[:, :k]
    for c in range(EARLY, chunks):
        send_deb(c)

    loads[4].wait()
    loads[5].wait()
    writes = []

    def write(src, dst):
        copy = pltpu.make_async_copy(src, dst, write_sem.at[len(writes)])
        copy.start()
        writes.append(copy)

    def moments(c):
        g_copies[c].wait_recv()
        here = part[c]
        grad = g_own[here, :] + g_far[here, :].astype(F32)
        first = 0.9 * m1[here, :] + 0.1 * grad
        second = 0.95 * m2[here, :] + 0.05 * grad * grad
        value = num[here, :]
        plain = value / jnp.full((1, 1), weight, F32)
        mine = value - 0.001 * (first / (jnp.sqrt(second) + 1e-08) + 0.1 * plain)
        half_send[here, :] = mine.astype(BF16)
        half_copies[c].start()
        half[here, :] = mine
        m1[here, :] = first
        m2[here, :] = second
        write(m1.at[here], m1o_hbm.at[0, here])
        write(m2.at[here], m2o_hbm.at[0, here])

    def forward(c):
        deb_copies[c].wait_recv()
        here = part[c]
        deb2 = jnp.concatenate([deb_own[here, :], deb_far[here, :]], axis=1)
        dims = (((1,), (1,)), ((), ()))
        both = jnp.concatenate([cot_own[pl.ds(rows, rows), :], cot_far[pl.ds(rows, rows), :]], axis=1)
        gn_send[c] = lax.dot_general(both, deb2, dims, preferred_element_type=F32).astype(BF16)
        gn_copies[c].start()
        product = jnp.dot(nrm[c], deb2, preferred_element_type=F32)
        if c:
            product = val_acc[...] + product
        if c < chunks - 1:
            val_acc[...] = product
        else:
            val_send[...] = product[:, k:].astype(BF16)
            for copy in val_copies:
                copy.start()
            val_own[...] = product[:, :k].astype(BF16)
            write(val_own.at[pl.ds(0, rows)], val_hbm.at[row_block(tp)])
            write(val_own.at[pl.ds(rows, rows)], val_hbm.at[row_block(near)])
        both = jnp.concatenate([cot_own[pl.ds(0, rows), :], cot_far[pl.ds(0, rows), :]], axis=1)
        gn[c] = lax.dot_general(both, deb2, dims, preferred_element_type=F32)

    for c in range(chunks):
        moments(c)
    for c in range(chunks):
        forward(c)

    inner = jnp.zeros((rows, 1), F32)
    for c in range(chunks):
        gn_copies[c].wait_recv()
        total = gn[c] + gn_near[c].astype(F32)
        gn[c] = total
        normal = hid[:, c * fc:(c + 1) * fc].astype(F32) * scale[...]
        inner = inner + jnp.sum(total * normal, axis=1, keepdims=True)
    inner = inner / width
    for c in range(chunks):
        s = scale[...]
        normal = hid[:, c * fc:(c + 1) * fc].astype(F32) * s
        gh[:, c * fc:(c + 1) * fc] = (s * (gn[c] - normal * inner)).astype(BF16)
    write(gh, gh_hbm)

    for c in range(chunks):
        half_copies[c].wait_recv()
        here = part[c]
        num[here, :] = 0.5 * (half[here, :] + half_far[here, :].astype(F32))
        write(num.at[here], numo_hbm.at[0, here])
    w_copy.wait_recv()
    wo_ref[0] = 0.5 * (weight + jnp.max(w_far[...]))

    for copy in val_copies:
        copy.wait_recv()
    for group in (cot_copies, nrm_copies, deb_copies, g_copies, half_copies, gn_copies, val_copies, [w_copy]):
        for copy in group:
            copy.wait_send()
    for copy in writes:
        copy.wait()


def step_of(dist, level, chunks, operands):
    _, hidden, cotangent, numerator, moment_one, moment_two = operands
    rows, width = hidden.shape
    tokens, k = cotangent.shape
    fc = width // chunks
    any_space = pl.BlockSpec(memory_space=pl.ANY)
    smem = pl.BlockSpec(memory_space=pltpu.SMEM)
    dma = pltpu.SemaphoreType.DMA
    full32, full16 = pltpu.VMEM((width, k), F32), pltpu.VMEM((width, k), BF16)
    tok16 = pltpu.VMEM((2 * rows, k), BF16)
    small = pltpu.VMEM((8, 128), F32)
    shapes = [
        jax.ShapeDtypeStruct(numerator.shape, F32),
        jax.ShapeDtypeStruct((1,), F32),
        jax.ShapeDtypeStruct(moment_one.shape, F32),
        jax.ShapeDtypeStruct(moment_two.shape, F32),
        jax.ShapeDtypeStruct((tokens, k), BF16),
        jax.ShapeDtypeStruct((rows, width), BF16),
    ]
    scratch = [
        pltpu.VMEM((rows, width), BF16), full32, full32, full32, tok16, tok16,
        pltpu.VMEM((chunks, 2 * rows, fc), BF16), pltpu.VMEM((rows, 1), F32),
        full16, full16, full32, full16, full16, full32, full16, full16,
        pltpu.VMEM((chunks, rows, fc), F32), pltpu.VMEM((chunks, rows, fc), BF16),
        pltpu.VMEM((chunks, rows, fc), BF16), pltpu.VMEM((rows, width), BF16),
        pltpu.VMEM((2 * rows, 2 * k), F32), tok16, tok16, small, small,
        dma((6,)), dma((3 * chunks + 3,)),
        dma((2,)), dma((2,)),
    ] + [dma((chunks,))] * 10 + [dma((2,)), dma((2,)), dma((1,)), dma((1,))]
    return pl.pallas_call(
        functools.partial(kernel, dist, chunks),
        out_shape=shapes,
        in_specs=[smem] + [any_space] * 5,
        out_specs=[any_space, smem] + [any_space] * 4,
        scratch_shapes=scratch,
        compiler_params=pltpu.CompilerParams(
            collective_id=level, has_side_effects=True, vmem_limit_bytes=48 * 1024 * 1024
        ),
        cost_estimate=pl.CostEstimate(flops=12 * rows * width * 2 * k, bytes_accessed=12_000_000, transcendentals=0),
    )(*operands)


def local(hidden, cotangent, numerator, push_weight, moment_one, moment_two, gossip_round):
    operands = (push_weight, hidden, cotangent, numerator, moment_one, moment_two)
    branches = [
        (lambda items, level=level: tuple(step_of(2**level, level, CHUNKS, items))) for level in range(ROUNDS)
    ]
    return lax.switch(gossip_round[0], branches, operands)


def solution(mesh):
    placed = (
        P(("rep", "tp"), None),
        P("rep", "tp"),
        P("rep", None, "tp"),
        P("rep"),
        P("rep", None, "tp"),
        P("rep", None, "tp"),
        P(),
    )
    return jax.shard_map(
        local,
        mesh=mesh,
        in_specs=placed,
        out_specs=(
            P("rep", None, "tp"),
            P("rep"),
            P("rep", None, "tp"),
            P("rep", None, "tp"),
            P("rep", "tp"),
            P(("rep", "tp"), None),
        ),
        check_vma=False,
    )
```

```python
import functools

import jax
import jax.numpy as jnp
from jax import lax
from jax.experimental import pallas as pl
from jax.experimental.pallas import tpu as pltpu
from jax.sharding import PartitionSpec as P

MESH = pl.DeviceIdType.MESH
F32 = jnp.float32
BF16 = jnp.bfloat16
ROUNDS = 3
CHUNKS = 10
EARLY = 2


def kernel(
    dist, chunks,
    w_ref, hid_hbm, cot_hbm, num_hbm, m1_hbm, m2_hbm,
    numo_hbm, wo_ref, m1o_hbm, m2o_hbm, val_hbm, gh_hbm,
    hid, num, m1, m2, cot_own, cot_far, nrm, scale,
    deb_own, deb_far, g_own, g_send, g_far, half, half_send, half_far,
    gn, gn_send, gn_near, gh, val_acc, val_own, val_send, w_send, w_far,
    load_sem, write_sem,
    cot_s, cot_r, nrm_s, nrm_r, deb_s, deb_r, g_s, g_r, half_s, half_r, gn_s, gn_r, val_s, val_r, w_s, w_r,
):
    rows, width = hid.shape
    fc = width // chunks
    rep, tp = lax.axis_index("rep"), lax.axis_index("tp")
    n_rep = lax.axis_size("rep")
    near = tp + 1 - 2 * lax.rem(tp, 2)
    far = lax.rem(tp + 2, 4)
    far_near = lax.rem(near + 2, 4)
    to_rep = lax.rem(rep + dist, n_rep)
    from_rep = lax.rem(rep + n_rep - dist, n_rep)
    near_dev, far_dev, to_dev, from_dev = (rep, near), (rep, far), (to_rep, tp), (from_rep, tp)

    def row_block(index):
        return pl.ds(pl.multiple_of(index * rows, rows), rows)

    barrier = pltpu.get_barrier_semaphore()
    for device in (near_dev, far_dev, to_dev, from_dev):
        pl.semaphore_signal(barrier, inc=1, device_id=device, device_id_type=MESH)
    loads = [
        pltpu.make_async_copy(num_hbm.at[0], num, load_sem.at[1]),
        pltpu.make_async_copy(hid_hbm, hid, load_sem.at[0]),
        pltpu.make_async_copy(cot_hbm.at[row_block(tp)], cot_own.at[pl.ds(0, rows)], load_sem.at[2]),
        pltpu.make_async_copy(cot_hbm.at[row_block(near)], cot_own.at[pl.ds(rows, rows)], load_sem.at[3]),
        pltpu.make_async_copy(m1_hbm.at[0], m1, load_sem.at[4]),
        pltpu.make_async_copy(m2_hbm.at[0], m2, load_sem.at[5]),
    ]
    for load in loads:
        load.start()
    weight = w_ref[0]
    w_send[...] = jnp.full(w_send.shape, weight, F32)
    part = [pl.ds(c * fc, fc) for c in range(chunks)]
    loads[0].wait()
    for here in part:
        deb_own[here, :] = (num[here, :] / jnp.full((1, 1), weight, F32)).astype(BF16)
    pl.semaphore_wait(barrier, 4)

    def remote(src, dst, send, recv, device):
        return pltpu.make_async_remote_copy(
            src_ref=src, dst_ref=dst, send_sem=send, recv_sem=recv, device_id=device, device_id_type=MESH
        )

    cot_copies = [
        remote(cot_hbm.at[row_block(far)], cot_far.at[pl.ds(0, rows)], cot_s.at[0], cot_r.at[0], far_dev),
        remote(cot_hbm.at[row_block(far_near)], cot_far.at[pl.ds(rows, rows)], cot_s.at[1], cot_r.at[1], far_dev),
    ]
    for copy in cot_copies:
        copy.start()
    nrm_copies = [
        remote(nrm.at[c, pl.ds(0, rows)], nrm.at[c, pl.ds(rows, rows)], nrm_s.at[c], nrm_r.at[c], near_dev)
        for c in range(chunks)
    ]
    deb_copies = [
        remote(deb_own.at[part[c]], deb_far.at[part[c]], deb_s.at[c], deb_r.at[c], far_dev) for c in range(chunks)
    ]
    g_copies = [
        remote(g_send.at[part[c]], g_far.at[part[c]], g_s.at[c], g_r.at[c], far_dev) for c in range(chunks)
    ]
    half_copies = [
        remote(half_send.at[part[c]], half_far.at[part[c]], half_s.at[c], half_r.at[c], to_dev)
        for c in range(chunks)
    ]
    gn_copies = [
        remote(gn_send.at[c], gn_near.at[c], gn_s.at[c], gn_r.at[c], near_dev) for c in range(chunks)
    ]
    val_copies = [
        remote(val_send.at[pl.ds(0, rows)], val_hbm.at[row_block(tp)], val_s.at[0], val_r.at[0], far_dev),
        remote(val_send.at[pl.ds(rows, rows)], val_hbm.at[row_block(near)], val_s.at[1], val_r.at[1], far_dev),
    ]
    for copy in deb_copies[:EARLY]:
        copy.start()
    w_copy = remote(w_send, w_far, w_s.at[0], w_r.at[0], to_dev)
    w_copy.start()

    loads[1].wait()
    step = 32

    @pl.loop(0, rows // step)
    def _(block):
        here = pl.ds(pl.multiple_of(block * step, step), step)
        x = hid[here, :].astype(F32)
        s = lax.rsqrt(jnp.mean(x * x, axis=1, keepdims=True) + 1e-06)
        scale[here, :] = s
        y = (x * s).astype(BF16)
        for c in range(chunks):
            nrm[c, here, :] = y[:, c * fc:(c + 1) * fc]

    for copy in nrm_copies:
        copy.start()

    loads[2].wait()
    loads[3].wait()
    for copy in cot_copies:
        copy.wait_recv()
    cot2 = jnp.concatenate([cot_own[...], cot_far[...]], axis=1)
    k = cot_own.shape[1]
    for c in range(chunks):
        nrm_copies[c].wait_recv()
        p = lax.dot_general(nrm[c], cot2, (((0,), (0,)), ((), ())), preferred_element_type=F32)
        g_send[part[c], :] = p[:, k:].astype(BF16)
        g_copies[c].start()
        g_own[part[c], :] = p[:, :k]
    for copy in deb_copies[EARLY:]:
        copy.start()

    loads[4].wait()
    loads[5].wait()
    writes = []

    def write(src, dst):
        copy = pltpu.make_async_copy(src, dst, write_sem.at[len(writes)])
        copy.start()
        writes.append(copy)

    def moments(c):
        g_copies[c].wait_recv()
        here = part[c]
        grad = g_own[here, :] + g_far[here, :].astype(F32)
        first = 0.9 * m1[here, :] + 0.1 * grad
        second = 0.95 * m2[here, :] + 0.05 * grad * grad
        value = num[here, :]
        plain = value / jnp.full((1, 1), weight, F32)
        mine = value - 0.001 * (first / (jnp.sqrt(second) + 1e-08) + 0.1 * plain)
        half_send[here, :] = mine.astype(BF16)
        half_copies[c].start()
        half[here, :] = mine
        m1[here, :] = first
        m2[here, :] = second
        write(m1.at[here], m1o_hbm.at[0, here])
        write(m2.at[here], m2o_hbm.at[0, here])

    def forward(c):
        deb_copies[c].wait_recv()
        here = part[c]
        deb2 = jnp.concatenate([deb_own[here, :], deb_far[here, :]], axis=1)
        dims = (((1,), (1,)), ((), ()))
        both = jnp.concatenate([cot_own[pl.ds(rows, rows), :], cot_far[pl.ds(rows, rows), :]], axis=1)
        gn_send[c] = lax.dot_general(both, deb2, dims, preferred_element_type=F32).astype(BF16)
        gn_copies[c].start()
        product = jnp.dot(nrm[c], deb2, preferred_element_type=F32)
        if c:
            product = val_acc[...] + product
        if c < chunks - 1:
            val_acc[...] = product
        else:
            val_send[...] = product[:, k:].astype(BF16)
            for copy in val_copies:
                copy.start()
            val_own[...] = product[:, :k].astype(BF16)
            write(val_own.at[pl.ds(0, rows)], val_hbm.at[row_block(tp)])
            write(val_own.at[pl.ds(rows, rows)], val_hbm.at[row_block(near)])
        both = jnp.concatenate([cot_own[pl.ds(0, rows), :], cot_far[pl.ds(0, rows), :]], axis=1)
        gn[c] = lax.dot_general(both, deb2, dims, preferred_element_type=F32)

    for c in range(chunks):
        moments(c)
    for c in range(chunks):
        forward(c)

    def mix(c):
        half_copies[c].wait_recv()
        here = part[c]
        num[here, :] = 0.5 * (half[here, :] + half_far[here, :].astype(F32))
        write(num.at[here], numo_hbm.at[0, here])

    lead = chunks // 2
    for c in range(lead):
        mix(c)
    inner = jnp.zeros((rows, 1), F32)
    for c in range(chunks):
        gn_copies[c].wait_recv()
        total = gn[c] + gn_near[c].astype(F32)
        gn[c] = total
        normal = hid[:, c * fc:(c + 1) * fc].astype(F32) * scale[...]
        inner = inner + jnp.sum(total * normal, axis=1, keepdims=True)
    inner = inner / width
    quarter = rows // 4
    for q in range(4):
        some = pl.ds(q * quarter, quarter)
        s = scale[some, :]
        mean = inner[q * quarter:(q + 1) * quarter]
        for c in range(chunks):
            normal = hid[some, c * fc:(c + 1) * fc].astype(F32) * s
            gh[some, c * fc:(c + 1) * fc] = (s * (gn[c, some, :] - normal * mean)).astype(BF16)
        write(gh.at[some], gh_hbm.at[some])
    for c in range(lead, chunks):
        mix(c)
    w_copy.wait_recv()
    wo_ref[0] = 0.5 * (weight + jnp.max(w_far[...]))

    for copy in val_copies:
        copy.wait_recv()
    for group in (cot_copies, nrm_copies, deb_copies, g_copies, half_copies, gn_copies, val_copies, [w_copy]):
        for copy in group:
            copy.wait_send()
    for copy in writes:
        copy.wait()


def step_of(dist, level, chunks, operands):
    _, hidden, cotangent, numerator, moment_one, moment_two = operands
    rows, width = hidden.shape
    tokens, k = cotangent.shape
    fc = width // chunks
    any_space = pl.BlockSpec(memory_space=pl.ANY)
    smem = pl.BlockSpec(memory_space=pltpu.SMEM)
    dma = pltpu.SemaphoreType.DMA
    full32, full16 = pltpu.VMEM((width, k), F32), pltpu.VMEM((width, k), BF16)
    tok16 = pltpu.VMEM((2 * rows, k), BF16)
    small = pltpu.VMEM((8, 128), F32)
    shapes = [
        jax.ShapeDtypeStruct(numerator.shape, F32),
        jax.ShapeDtypeStruct((1,), F32),
        jax.ShapeDtypeStruct(moment_one.shape, F32),
        jax.ShapeDtypeStruct(moment_two.shape, F32),
        jax.ShapeDtypeStruct((tokens, k), BF16),
        jax.ShapeDtypeStruct((rows, width), BF16),
    ]
    scratch = [
        pltpu.VMEM((rows, width), BF16), full32, full32, full32, tok16, tok16,
        pltpu.VMEM((chunks, 2 * rows, fc), BF16), pltpu.VMEM((rows, 1), F32),
        full16, full16, full32, full16, full16, full32, full16, full16,
        pltpu.VMEM((chunks, rows, fc), F32), pltpu.VMEM((chunks, rows, fc), BF16),
        pltpu.VMEM((chunks, rows, fc), BF16), pltpu.VMEM((rows, width), BF16),
        pltpu.VMEM((2 * rows, 2 * k), F32), tok16, tok16, small, small,
        dma((6,)), dma((3 * chunks + 6,)),
        dma((2,)), dma((2,)),
    ] + [dma((chunks,))] * 10 + [dma((2,)), dma((2,)), dma((1,)), dma((1,))]
    return pl.pallas_call(
        functools.partial(kernel, dist, chunks),
        out_shape=shapes,
        in_specs=[smem] + [any_space] * 5,
        out_specs=[any_space, smem] + [any_space] * 4,
        scratch_shapes=scratch,
        compiler_params=pltpu.CompilerParams(
            collective_id=level, has_side_effects=True, vmem_limit_bytes=48 * 1024 * 1024
        ),
        cost_estimate=pl.CostEstimate(flops=12 * rows * width * 2 * k, bytes_accessed=12_000_000, transcendentals=0),
    )(*operands)


def place_kernel(pieces, count, *refs):
    sources, targets, sem = refs[:count], refs[count:2 * count], refs[2 * count]
    copies = []
    for source, target in zip(sources, targets):
        size = source.shape[-2] // pieces
        for piece in range(pieces):
            some = pl.ds(piece * size, size)
            at = (0, some) if len(source.shape) == 3 else (some,)
            copies.append(pltpu.make_async_copy(source.at[at], target.at[at], sem.at[len(copies)]))
            copies[-1].start()
    for copy in copies:
        copy.wait()


def place(arrays, pieces=4):
    count = len(arrays)
    any_space = pl.BlockSpec(memory_space=pl.ANY)
    return pl.pallas_call(
        functools.partial(place_kernel, pieces, count),
        out_shape=[jax.ShapeDtypeStruct(a.shape, a.dtype) for a in arrays],
        in_specs=[any_space] * count,
        out_specs=[any_space] * count,
        scratch_shapes=[pltpu.SemaphoreType.DMA((pieces * count,))],
        compiler_params=pltpu.CompilerParams(vmem_limit_bytes=1024 * 1024),
    )(*arrays)


def local(hidden, cotangent, numerator, push_weight, moment_one, moment_two, gossip_round):
    operands = (push_weight, hidden, cotangent, numerator, moment_one, moment_two)
    branches = [
        (lambda items, level=level: tuple(step_of(2**level, level, CHUNKS, items))) for level in range(ROUNDS)
    ]
    numerator_out, weight_out, *others = lax.switch(gossip_round[0], branches, operands)
    numerator_out, first, second, values, grad_hidden = place([numerator_out, *others])
    return numerator_out, weight_out, first, second, values, grad_hidden


def solution(mesh):
    placed = (
        P(("rep", "tp"), None),
        P("rep", "tp"),
        P("rep", None, "tp"),
        P("rep"),
        P("rep", None, "tp"),
        P("rep", None, "tp"),
        P(),
    )
    return jax.shard_map(
        local,
        mesh=mesh,
        in_specs=placed,
        out_specs=(
            P("rep", None, "tp"),
            P("rep"),
            P("rep", None, "tp"),
            P("rep", None, "tp"),
            P("rep", "tp"),
            P(("rep", "tp"), None),
        ),
        check_vma=False,
    )
```

```python
import functools

import jax
import jax.numpy as jnp
from jax import lax
from jax.experimental import pallas as pl
from jax.experimental.pallas import tpu as pltpu
from jax.sharding import PartitionSpec as P

MESH = pl.DeviceIdType.MESH
F32 = jnp.float32
BF16 = jnp.bfloat16
ROUNDS = 3
CHUNKS = 5


def kernel(
    dist, chunks,
    w_ref, hid_hbm, cot_hbm, num_hbm, m1_hbm, m2_hbm,
    numo_hbm, wo_ref, m1o_hbm, m2o_hbm, val_hbm, gh_hbm,
    hid, num, m1, m2, cot_own, cot_far, nrm, scale,
    deb_own, deb_far, g_own, g_send, g_far, half, half_send, half_far,
    gn, gn_send, gn_near, gh, val_acc, val_own, val_send, w_send, w_far,
    load_sem, write_sem,
    cot_s, cot_r, nrm_s, nrm_r, deb_s, deb_r, g_s, g_r, half_s, half_r, gn_s, gn_r, val_s, val_r, w_s, w_r,
):
    rows, width = hid.shape
    fc = width // chunks
    rep, tp = lax.axis_index("rep"), lax.axis_index("tp")
    n_rep = lax.axis_size("rep")
    near = tp + 1 - 2 * lax.rem(tp, 2)
    far = lax.rem(tp + 2, 4)
    far_near = lax.rem(near + 2, 4)
    to_rep = lax.rem(rep + dist, n_rep)
    from_rep = lax.rem(rep + n_rep - dist, n_rep)
    near_dev, far_dev, to_dev, from_dev = (rep, near), (rep, far), (to_rep, tp), (from_rep, tp)

    def row_block(index):
        return pl.ds(pl.multiple_of(index * rows, rows), rows)

    barrier = pltpu.get_barrier_semaphore()
    for device in (near_dev, far_dev, to_dev, from_dev):
        pl.semaphore_signal(barrier, inc=1, device_id=device, device_id_type=MESH)
    loads = [
        pltpu.make_async_copy(hid_hbm, hid, load_sem.at[0]),
        pltpu.make_async_copy(num_hbm.at[0], num, load_sem.at[1]),
        pltpu.make_async_copy(cot_hbm.at[row_block(tp)], cot_own.at[pl.ds(0, rows)], load_sem.at[2]),
        pltpu.make_async_copy(cot_hbm.at[row_block(near)], cot_own.at[pl.ds(rows, rows)], load_sem.at[3]),
        pltpu.make_async_copy(m1_hbm.at[0], m1, load_sem.at[4]),
        pltpu.make_async_copy(m2_hbm.at[0], m2, load_sem.at[5]),
    ]
    for load in loads:
        load.start()
    weight = w_ref[0]
    w_send[...] = jnp.full(w_send.shape, weight, F32)
    part = [pl.ds(c * fc, fc) for c in range(chunks)]
    pl.semaphore_wait(barrier, 4)

    def remote(src, dst, send, recv, device):
        return pltpu.make_async_remote_copy(
            src_ref=src, dst_ref=dst, send_sem=send, recv_sem=recv, device_id=device, device_id_type=MESH
        )

    cot_copies = [
        remote(cot_hbm.at[row_block(far)], cot_far.at[pl.ds(0, rows)], cot_s.at[0], cot_r.at[0], far_dev),
        remote(cot_hbm.at[row_block(far_near)], cot_far.at[pl.ds(rows, rows)], cot_s.at[1], cot_r.at[1], far_dev),
    ]
    for copy in cot_copies:
        copy.start()
    nrm_copies = [
        remote(nrm.at[c, pl.ds(0, rows)], nrm.at[c, pl.ds(rows, rows)], nrm_s.at[c], nrm_r.at[c], near_dev)
        for c in range(chunks)
    ]
    deb_copies = [
        remote(deb_own.at[part[c]], deb_far.at[part[c]], deb_s.at[c], deb_r.at[c], far_dev) for c in range(chunks)
    ]
    g_copies = [
        remote(g_send.at[part[c]], g_far.at[part[c]], g_s.at[c], g_r.at[c], far_dev) for c in range(chunks)
    ]
    half_copies = [
        remote(half_send.at[part[c]], half_far.at[part[c]], half_s.at[c], half_r.at[c], to_dev)
        for c in range(chunks)
    ]
    gn_copies = [
        remote(gn_send.at[c], gn_near.at[c], gn_s.at[c], gn_r.at[c], near_dev) for c in range(chunks)
    ]
    val_copies = [
        remote(val_send.at[pl.ds(0, rows)], val_hbm.at[row_block(tp)], val_s.at[0], val_r.at[0], far_dev),
        remote(val_send.at[pl.ds(rows, rows)], val_hbm.at[row_block(near)], val_s.at[1], val_r.at[1], far_dev),
    ]
    w_copy = remote(w_send, w_far, w_s.at[0], w_r.at[0], to_dev)
    w_copy.start()

    loads[0].wait()
    step = 32

    @pl.loop(0, rows // step)
    def _(block):
        here = pl.ds(pl.multiple_of(block * step, step), step)
        x = hid[here, :].astype(F32)
        s = lax.rsqrt(jnp.mean(x * x, axis=1, keepdims=True) + 1e-06)
        scale[here, :] = s
        y = (x * s).astype(BF16)
        for c in range(chunks):
            nrm[c, here, :] = y[:, c * fc:(c + 1) * fc]

    for copy in nrm_copies:
        copy.start()

    loads[1].wait()

    def send_deb(c):
        deb_own[part[c], :] = (num[part[c], :] / jnp.full((1, 1), weight, F32)).astype(BF16)
        deb_copies[c].start()

    send_deb(0)
    loads[2].wait()
    loads[3].wait()
    for copy in cot_copies:
        copy.wait_recv()
    cot2 = jnp.concatenate([cot_own[...], cot_far[...]], axis=1)
    k = cot_own.shape[1]
    for c in range(chunks):
        nrm_copies[c].wait_recv()
        p = lax.dot_general(nrm[c], cot2, (((0,), (0,)), ((), ())), preferred_element_type=F32)
        g_send[part[c], :] = p[:, k:].astype(BF16)
        g_copies[c].start()
        if c < chunks - 1:
            send_deb(c + 1)
        g_own[part[c], :] = p[:, :k]

    loads[4].wait()
    loads[5].wait()
    writes = []

    def write(src, dst):
        copy = pltpu.make_async_copy(src, dst, write_sem.at[len(writes)])
        copy.start()
        writes.append(copy)

    def moments(c):
        g_copies[c].wait_recv()
        here = part[c]
        grad = g_own[here, :] + g_far[here, :].astype(F32)
        first = 0.9 * m1[here, :] + 0.1 * grad
        second = 0.95 * m2[here, :] + 0.05 * grad * grad
        value = num[here, :]
        plain = value / jnp.full((1, 1), weight, F32)
        mine = value - 0.001 * (first / (jnp.sqrt(second) + 1e-08) + 0.1 * plain)
        half_send[here, :] = mine.astype(BF16)
        half_copies[c].start()
        half[here, :] = mine
        m1[here, :] = first
        m2[here, :] = second
        write(m1.at[here], m1o_hbm.at[0, here])
        write(m2.at[here], m2o_hbm.at[0, here])

    def forward(c):
        deb_copies[c].wait_recv()
        here = part[c]
        deb2 = jnp.concatenate([deb_own[here, :], deb_far[here, :]], axis=1)
        dims = (((1,), (1,)), ((), ()))
        both = jnp.concatenate([cot_own[pl.ds(rows, rows), :], cot_far[pl.ds(rows, rows), :]], axis=1)
        gn_send[c] = lax.dot_general(both, deb2, dims, preferred_element_type=F32).astype(BF16)
        gn_copies[c].start()
        product = jnp.dot(nrm[c], deb2, preferred_element_type=F32)
        if c:
            product = val_acc[...] + product
        if c < chunks - 1:
            val_acc[...] = product
        else:
            val_send[...] = product[:, k:].astype(BF16)
            for copy in val_copies:
                copy.start()
            val_own[...] = product[:, :k].astype(BF16)
            write(val_own.at[pl.ds(0, rows)], val_hbm.at[row_block(tp)])
            write(val_own.at[pl.ds(rows, rows)], val_hbm.at[row_block(near)])
        both = jnp.concatenate([cot_own[pl.ds(0, rows), :], cot_far[pl.ds(0, rows), :]], axis=1)
        gn[c] = lax.dot_general(both, deb2, dims, preferred_element_type=F32)

    for c in range(chunks - 1):
        moments(c)
        forward(c)
    forward(chunks - 1)
    moments(chunks - 1)

    def mix(c):
        half_copies[c].wait_recv()
        here = part[c]
        num[here, :] = 0.5 * (half[here, :] + half_far[here, :].astype(F32))
        write(num.at[here], numo_hbm.at[0, here])

    lead = chunks // 2
    for c in range(lead):
        mix(c)
    inner = jnp.zeros((rows, 1), F32)
    for c in range(chunks):
        gn_copies[c].wait_recv()
        total = gn[c] + gn_near[c].astype(F32)
        gn[c] = total
        normal = hid[:, c * fc:(c + 1) * fc].astype(F32) * scale[...]
        inner = inner + jnp.sum(total * normal, axis=1, keepdims=True)
    inner = inner / width
    quarter = rows // 4
    for q in range(4):
        some = pl.ds(q * quarter, quarter)
        s = scale[some, :]
        mean = inner[q * quarter:(q + 1) * quarter]
        for c in range(chunks):
            normal = hid[some, c * fc:(c + 1) * fc].astype(F32) * s
            gh[some, c * fc:(c + 1) * fc] = (s * (gn[c, some, :] - normal * mean)).astype(BF16)
        write(gh.at[some], gh_hbm.at[some])
    for c in range(lead, chunks):
        mix(c)
    w_copy.wait_recv()
    wo_ref[0] = 0.5 * (weight + jnp.max(w_far[...]))

    for copy in val_copies:
        copy.wait_recv()
    for group in (cot_copies, nrm_copies, deb_copies, g_copies, half_copies, gn_copies, val_copies, [w_copy]):
        for copy in group:
            copy.wait_send()
    for copy in writes:
        copy.wait()


def step_of(dist, level, chunks, operands):
    _, hidden, cotangent, numerator, moment_one, moment_two = operands
    rows, width = hidden.shape
    tokens, k = cotangent.shape
    fc = width // chunks
    any_space = pl.BlockSpec(memory_space=pl.ANY)
    smem = pl.BlockSpec(memory_space=pltpu.SMEM)
    dma = pltpu.SemaphoreType.DMA
    full32, full16 = pltpu.VMEM((width, k), F32), pltpu.VMEM((width, k), BF16)
    tok16 = pltpu.VMEM((2 * rows, k), BF16)
    small = pltpu.VMEM((8, 128), F32)
    shapes = [
        jax.ShapeDtypeStruct(numerator.shape, F32),
        jax.ShapeDtypeStruct((1,), F32),
        jax.ShapeDtypeStruct(moment_one.shape, F32),
        jax.ShapeDtypeStruct(moment_two.shape, F32),
        jax.ShapeDtypeStruct((tokens, k), BF16),
        jax.ShapeDtypeStruct((rows, width), BF16),
    ]
    scratch = [
        pltpu.VMEM((rows, width), BF16), full32, full32, full32, tok16, tok16,
        pltpu.VMEM((chunks, 2 * rows, fc), BF16), pltpu.VMEM((rows, 1), F32),
        full16, full16, full32, full16, full16, full32, full16, full16,
        pltpu.VMEM((chunks, rows, fc), F32), pltpu.VMEM((chunks, rows, fc), BF16),
        pltpu.VMEM((chunks, rows, fc), BF16), pltpu.VMEM((rows, width), BF16),
        pltpu.VMEM((2 * rows, 2 * k), F32), tok16, tok16, small, small,
        dma((6,)), dma((3 * chunks + 6,)),
        dma((2,)), dma((2,)),
    ] + [dma((chunks,))] * 10 + [dma((2,)), dma((2,)), dma((1,)), dma((1,))]
    return pl.pallas_call(
        functools.partial(kernel, dist, chunks),
        out_shape=shapes,
        in_specs=[smem] + [any_space] * 5,
        out_specs=[any_space, smem] + [any_space] * 4,
        scratch_shapes=scratch,
        compiler_params=pltpu.CompilerParams(
            collective_id=level, has_side_effects=True, vmem_limit_bytes=48 * 1024 * 1024
        ),
        cost_estimate=pl.CostEstimate(flops=12 * rows * width * 2 * k, bytes_accessed=12_000_000, transcendentals=0),
    )(*operands)


def place_kernel(pieces, count, *refs):
    sources, targets, stages = refs[:count], refs[count:2 * count], refs[2 * count:3 * count]
    in_sem, out_sem = refs[3 * count:]
    steps = []
    for source, stage, target in zip(sources, stages, targets):
        size = source.shape[-2] // pieces
        for piece in range(pieces):
            some = pl.ds(piece * size, size)
            at = (0, some) if len(source.shape) == 3 else (some,)
            index = len(steps)
            steps.append((
                pltpu.make_async_copy(source.at[at], stage.at[at], in_sem.at[index]),
                pltpu.make_async_copy(stage.at[at], target.at[at], out_sem.at[index]),
            ))
    for arrive, _ in steps:
        arrive.start()
    for arrive, leave in steps:
        arrive.wait()
        leave.start()
    for _, leave in steps:
        leave.wait()


def place(arrays, pieces=2):
    count = len(arrays)
    any_space = pl.BlockSpec(memory_space=pl.ANY)
    sems = pltpu.SemaphoreType.DMA((pieces * count,))
    return pl.pallas_call(
        functools.partial(place_kernel, pieces, count),
        out_shape=[jax.ShapeDtypeStruct(a.shape, a.dtype) for a in arrays],
        in_specs=[any_space] * count,
        out_specs=[any_space] * count,
        scratch_shapes=[pltpu.VMEM(a.shape, a.dtype) for a in arrays] + [sems, sems],
        compiler_params=pltpu.CompilerParams(vmem_limit_bytes=16 * 1024 * 1024),
    )(*arrays)


def local(hidden, cotangent, numerator, push_weight, moment_one, moment_two, gossip_round):
    operands = (push_weight, hidden, cotangent, numerator, moment_one, moment_two)
    branches = [
        (lambda items, level=level: tuple(step_of(2**level, level, CHUNKS, items))) for level in range(ROUNDS)
    ]
    numerator_out, weight_out, *others = lax.switch(gossip_round[0], branches, operands)
    numerator_out, first, second, values, grad_hidden = place([numerator_out, *others])
    return numerator_out, weight_out, first, second, values, grad_hidden


def solution(mesh):
    placed = (
        P(("rep", "tp"), None),
        P("rep", "tp"),
        P("rep", None, "tp"),
        P("rep"),
        P("rep", None, "tp"),
        P("rep", None, "tp"),
        P(),
    )
    return jax.shard_map(
        local,
        mesh=mesh,
        in_specs=placed,
        out_specs=(
            P("rep", None, "tp"),
            P("rep"),
            P("rep", None, "tp"),
            P("rep", None, "tp"),
            P("rep", "tp"),
            P(("rep", "tp"), None),
        ),
        check_vma=False,
    )
```

```python
import functools

import jax
import jax.numpy as jnp
from jax import lax
from jax.experimental import pallas as pl
from jax.experimental.pallas import tpu as pltpu
from jax.sharding import PartitionSpec as P

MESH = pl.DeviceIdType.MESH
F32 = jnp.float32
BF16 = jnp.bfloat16
ROUNDS = 3
CHUNKS = 10
EARLY = 3


def kernel(
    dist, chunks,
    w_ref, hid_hbm, cot_hbm, num_hbm, m1_hbm, m2_hbm,
    numo_hbm, wo_ref, m1o_hbm, m2o_hbm, val_hbm, gh_hbm,
    hid, num, m1, m2, cot_own, cot_far, nrm, scale,
    deb_own, deb_far, g_own, g_send, g_far, half, half_send, half_far,
    gn, gn_send, gn_near, gh, val_acc, val_own, val_send, w_send, w_far,
    load_sem, write_sem,
    cot_s, cot_r, nrm_s, nrm_r, deb_s, deb_r, g_s, g_r, half_s, half_r, gn_s, gn_r, val_s, val_r, w_s, w_r,
):
    rows, width = hid.shape
    fc = width // chunks
    rep, tp = lax.axis_index("rep"), lax.axis_index("tp")
    n_rep = lax.axis_size("rep")
    near = tp + 1 - 2 * lax.rem(tp, 2)
    far = lax.rem(tp + 2, 4)
    far_near = lax.rem(near + 2, 4)
    to_rep = lax.rem(rep + dist, n_rep)
    from_rep = lax.rem(rep + n_rep - dist, n_rep)
    near_dev, far_dev, to_dev, from_dev = (rep, near), (rep, far), (to_rep, tp), (from_rep, tp)

    def row_block(index):
        return pl.ds(pl.multiple_of(index * rows, rows), rows)

    barrier = pltpu.get_barrier_semaphore()
    for device in (near_dev, far_dev, to_dev, from_dev):
        pl.semaphore_signal(barrier, inc=1, device_id=device, device_id_type=MESH)
    loads = [
        pltpu.make_async_copy(num_hbm.at[0], num, load_sem.at[0]),
        pltpu.make_async_copy(hid_hbm, hid, load_sem.at[1]),
        pltpu.make_async_copy(cot_hbm.at[row_block(tp)], cot_own.at[pl.ds(0, rows)], load_sem.at[2]),
        pltpu.make_async_copy(cot_hbm.at[row_block(near)], cot_own.at[pl.ds(rows, rows)], load_sem.at[3]),
        pltpu.make_async_copy(m1_hbm.at[0], m1, load_sem.at[4]),
        pltpu.make_async_copy(m2_hbm.at[0], m2, load_sem.at[5]),
    ]
    for load in loads[:4]:
        load.start()
    weight = w_ref[0]
    w_send[...] = jnp.full(w_send.shape, weight, F32)
    part = [pl.ds(c * fc, fc) for c in range(chunks)]
    pl.semaphore_wait(barrier, 4)

    def remote(src, dst, send, recv, device):
        return pltpu.make_async_remote_copy(
            src_ref=src, dst_ref=dst, send_sem=send, recv_sem=recv, device_id=device, device_id_type=MESH
        )

    cot_copies = [
        remote(cot_hbm.at[row_block(far)], cot_far.at[pl.ds(0, rows)], cot_s.at[0], cot_r.at[0], far_dev),
        remote(cot_hbm.at[row_block(far_near)], cot_far.at[pl.ds(rows, rows)], cot_s.at[1], cot_r.at[1], far_dev),
    ]
    for copy in cot_copies:
        copy.start()
    nrm_copies = [
        remote(nrm.at[c, pl.ds(0, rows)], nrm.at[c, pl.ds(rows, rows)], nrm_s.at[c], nrm_r.at[c], near_dev)
        for c in range(chunks)
    ]
    deb_copies = [
        remote(deb_own.at[part[c]], deb_far.at[part[c]], deb_s.at[c], deb_r.at[c], far_dev) for c in range(chunks)
    ]
    g_copies = [
        remote(g_send.at[part[c]], g_far.at[part[c]], g_s.at[c], g_r.at[c], far_dev) for c in range(chunks)
    ]
    half_copies = [
        remote(half_send.at[part[c]], half_far.at[part[c]], half_s.at[c], half_r.at[c], to_dev)
        for c in range(chunks)
    ]
    gn_copies = [
        remote(gn_send.at[c], gn_near.at[c], gn_s.at[c], gn_r.at[c], near_dev) for c in range(chunks)
    ]
    val_copies = [
        remote(val_send.at[pl.ds(0, rows)], val_hbm.at[row_block(tp)], val_s.at[0], val_r.at[0], far_dev),
        remote(val_send.at[pl.ds(rows, rows)], val_hbm.at[row_block(near)], val_s.at[1], val_r.at[1], far_dev),
    ]
    w_copy = remote(w_send, w_far, w_s.at[0], w_r.at[0], to_dev)
    w_copy.start()

    def send_deb(c):
        deb_own[part[c], :] = (num[part[c], :] / jnp.full((1, 1), weight, F32)).astype(BF16)
        deb_copies[c].start()

    loads[0].wait()
    for c in range(EARLY):
        send_deb(c)
    loads[1].wait()
    step = 32

    @pl.loop(0, rows // step)
    def _(block):
        here = pl.ds(pl.multiple_of(block * step, step), step)
        x = hid[here, :].astype(F32)
        s = lax.rsqrt(jnp.mean(x * x, axis=1, keepdims=True) + 1e-06)
        scale[here, :] = s
        y = (x * s).astype(BF16)
        for c in range(chunks):
            nrm[c, here, :] = y[:, c * fc:(c + 1) * fc]

    for copy in nrm_copies:
        copy.start()

    for load in loads[4:]:
        load.start()
    loads[2].wait()
    loads[3].wait()
    for copy in cot_copies:
        copy.wait_recv()
    cot2 = jnp.concatenate([cot_own[...], cot_far[...]], axis=1)
    k = cot_own.shape[1]
    for c in range(chunks):
        nrm_copies[c].wait_recv()
        p = lax.dot_general(nrm[c], cot2, (((0,), (0,)), ((), ())), preferred_element_type=F32)
        g_send[part[c], :] = p[:, k:].astype(BF16)
        g_copies[c].start()
        g_own[part[c], :] = p[:, :k]
    for c in range(EARLY, chunks):
        send_deb(c)

    loads[4].wait()
    loads[5].wait()
    writes = []

    def write(src, dst):
        copy = pltpu.make_async_copy(src, dst, write_sem.at[len(writes)])
        copy.start()
        writes.append(copy)

    def moments(c):
        g_copies[c].wait_recv()
        here = part[c]
        grad = g_own[here, :] + g_far[here, :].astype(F32)
        first = 0.9 * m1[here, :] + 0.1 * grad
        second = 0.95 * m2[here, :] + 0.05 * grad * grad
        value = num[here, :]
        plain = value / jnp.full((1, 1), weight, F32)
        mine = value - 0.001 * (first / (jnp.sqrt(second) + 1e-08) + 0.1 * plain)
        half_send[here, :] = mine.astype(BF16)
        half_copies[c].start()
        half[here, :] = mine
        m1[here, :] = first
        m2[here, :] = second
        write(m1.at[here], m1o_hbm.at[0, here])
        write(m2.at[here], m2o_hbm.at[0, here])

    def swap_grad_normed(c, deb2):
        dims = (((1,), (1,)), ((), ()))
        both = jnp.concatenate([cot_own[pl.ds(rows, rows), :], cot_far[pl.ds(rows, rows), :]], axis=1)
        gn_send[c] = lax.dot_general(both, deb2, dims, preferred_element_type=F32).astype(BF16)
        gn_copies[c].start()
        both = jnp.concatenate([cot_own[pl.ds(0, rows), :], cot_far[pl.ds(0, rows), :]], axis=1)
        gn[c] = lax.dot_general(both, deb2, dims, preferred_element_type=F32)

    def forward(c):
        deb_copies[c].wait_recv()
        here = part[c]
        deb2 = jnp.concatenate([deb_own[here, :], deb_far[here, :]], axis=1)
        if c < chunks - 1:
            swap_grad_normed(c, deb2)
        product = jnp.dot(nrm[c], deb2, preferred_element_type=F32)
        if c:
            product = val_acc[...] + product
        if c < chunks - 1:
            val_acc[...] = product
        else:
            val_send[...] = product[:, k:].astype(BF16)
            for copy in val_copies:
                copy.start()
            swap_grad_normed(c, deb2)
            val_own[...] = product[:, :k].astype(BF16)
            write(val_own.at[pl.ds(0, rows)], val_hbm.at[row_block(tp)])
            write(val_own.at[pl.ds(rows, rows)], val_hbm.at[row_block(near)])

    def add_inner(c, inner):
        gn_copies[c].wait_recv()
        total = gn[c] + gn_near[c].astype(F32)
        gn[c] = total
        normal = hid[:, c * fc:(c + 1) * fc].astype(F32) * scale[...]
        return inner + jnp.sum(total * normal, axis=1, keepdims=True)

    def mix(c):
        half_copies[c].wait_recv()
        here = part[c]
        num[here, :] = 0.5 * (half[here, :] + half_far[here, :].astype(F32))
        write(num.at[here], numo_hbm.at[0, here])

    for c in range(chunks):
        moments(c)
    inner = jnp.zeros((rows, 1), F32)
    mixed = 0
    for c in range(chunks):
        forward(c)
        if c:
            inner = add_inner(c - 1, inner)
        ready = c if dist < 4 else c // 2
        while mixed < ready:
            mix(mixed)
            mixed += 1
    inner = add_inner(chunks - 1, inner) / width
    quarter = rows // 4
    for q in range(4):
        some = pl.ds(q * quarter, quarter)
        s = scale[some, :]
        mean = inner[q * quarter:(q + 1) * quarter]
        for c in range(chunks):
            normal = hid[some, c * fc:(c + 1) * fc].astype(F32) * s
            gh[some, c * fc:(c + 1) * fc] = (s * (gn[c, some, :] - normal * mean)).astype(BF16)
        write(gh.at[some], gh_hbm.at[some])
    for c in range(mixed, chunks):
        mix(c)
    w_copy.wait_recv()
    wo_ref[0] = 0.5 * (weight + jnp.max(w_far[...]))

    for copy in val_copies:
        copy.wait_recv()
    for group in (cot_copies, nrm_copies, deb_copies, g_copies, half_copies, gn_copies, val_copies, [w_copy]):
        for copy in group:
            copy.wait_send()
    for copy in writes:
        copy.wait()


def step_of(dist, level, chunks, operands):
    _, hidden, cotangent, numerator, moment_one, moment_two = operands
    rows, width = hidden.shape
    tokens, k = cotangent.shape
    fc = width // chunks
    any_space = pl.BlockSpec(memory_space=pl.ANY)
    smem = pl.BlockSpec(memory_space=pltpu.SMEM)
    dma = pltpu.SemaphoreType.DMA
    full32, full16 = pltpu.VMEM((width, k), F32), pltpu.VMEM((width, k), BF16)
    tok16 = pltpu.VMEM((2 * rows, k), BF16)
    small = pltpu.VMEM((8, 128), F32)
    shapes = [
        jax.ShapeDtypeStruct(numerator.shape, F32),
        jax.ShapeDtypeStruct((1,), F32),
        jax.ShapeDtypeStruct(moment_one.shape, F32),
        jax.ShapeDtypeStruct(moment_two.shape, F32),
        jax.ShapeDtypeStruct((tokens, k), BF16),
        jax.ShapeDtypeStruct((rows, width), BF16),
    ]
    scratch = [
        pltpu.VMEM((rows, width), BF16), full32, full32, full32, tok16, tok16,
        pltpu.VMEM((chunks, 2 * rows, fc), BF16), pltpu.VMEM((rows, 1), F32),
        full16, full16, full32, full16, full16, full32, full16, full16,
        pltpu.VMEM((chunks, rows, fc), F32), pltpu.VMEM((chunks, rows, fc), BF16),
        pltpu.VMEM((chunks, rows, fc), BF16), pltpu.VMEM((rows, width), BF16),
        pltpu.VMEM((2 * rows, 2 * k), F32), tok16, tok16, small, small,
        dma((6,)), dma((3 * chunks + 6,)),
        dma((2,)), dma((2,)),
    ] + [dma((chunks,))] * 10 + [dma((2,)), dma((2,)), dma((1,)), dma((1,))]
    return pl.pallas_call(
        functools.partial(kernel, dist, chunks),
        out_shape=shapes,
        in_specs=[smem] + [any_space] * 5,
        out_specs=[any_space, smem] + [any_space] * 4,
        scratch_shapes=scratch,
        compiler_params=pltpu.CompilerParams(
            collective_id=level, has_side_effects=True, vmem_limit_bytes=28 * 1024 * 1024
        ),
        cost_estimate=pl.CostEstimate(flops=12 * rows * width * 2 * k, bytes_accessed=12_000_000, transcendentals=0),
    )(*operands)


def place_kernel(pieces, count, *refs):
    sources, targets, sem = refs[:count], refs[count:2 * count], refs[2 * count]
    copies = []
    for source, target in zip(sources, targets):
        size = source.shape[-2] // pieces
        for piece in range(pieces):
            some = pl.ds(piece * size, size)
            at = (0, some) if len(source.shape) == 3 else (some,)
            copies.append(pltpu.make_async_copy(source.at[at], target.at[at], sem.at[len(copies)]))
            copies[-1].start()
    for copy in copies:
        copy.wait()


def place(arrays, pieces=2):
    count = len(arrays)
    return pl.pallas_call(
        functools.partial(place_kernel, pieces, count),
        out_shape=[jax.ShapeDtypeStruct(a.shape, a.dtype) for a in arrays],
        in_specs=[pl.BlockSpec(memory_space=pltpu.VMEM)] * count,
        out_specs=[pl.BlockSpec(memory_space=pl.ANY)] * count,
        scratch_shapes=[pltpu.SemaphoreType.DMA((pieces * count,))],
        compiler_params=pltpu.CompilerParams(vmem_limit_bytes=16 * 1024 * 1024),
    )(*arrays)


def local(hidden, cotangent, numerator, push_weight, moment_one, moment_two, gossip_round):
    operands = (push_weight, hidden, cotangent, numerator, moment_one, moment_two)
    branches = [
        (lambda items, level=level: tuple(step_of(2**level, level, CHUNKS, items))) for level in range(ROUNDS)
    ]
    numerator_out, weight_out, *others = lax.switch(gossip_round[0], branches, operands)
    numerator_out, first, second, values, grad_hidden = place([numerator_out, *others])
    return numerator_out, weight_out, first, second, values, grad_hidden


def solution(mesh):
    placed = (
        P(("rep", "tp"), None),
        P("rep", "tp"),
        P("rep", None, "tp"),
        P("rep"),
        P("rep", None, "tp"),
        P("rep", None, "tp"),
        P(),
    )
    return jax.shard_map(
        local,
        mesh=mesh,
        in_specs=placed,
        out_specs=(
            P("rep", None, "tp"),
            P("rep"),
            P("rep", None, "tp"),
            P("rep", None, "tp"),
            P("rep", "tp"),
            P(("rep", "tp"), None),
        ),
        check_vma=False,
    )
```

```python
import functools

import jax
import jax.numpy as jnp
from jax import lax
from jax.experimental import pallas as pl
from jax.experimental.pallas import tpu as pltpu
from jax.sharding import PartitionSpec as P

MESH = pl.DeviceIdType.MESH
F32 = jnp.float32
BF16 = jnp.bfloat16
ROUNDS = 3
CHUNKS = 5
EARLY = 1


def kernel(
    dist, chunks,
    w_ref, hid_hbm, cot_hbm, num_hbm, m1_hbm, m2_hbm,
    numo_hbm, wo_ref, m1o_hbm, m2o_hbm, val_hbm, gh_hbm,
    hid, num, m1, m2, cot_own, cot_far, nrm, scale,
    deb_own, deb_far, g_own, g_send, g_far, half, half_send, half_far,
    gn, gn_send, gn_near, gh, val_acc, val_own, val_send, w_send, w_far,
    load_sem, write_sem,
    cot_s, cot_r, nrm_s, nrm_r, deb_s, deb_r, g_s, g_r, half_s, half_r, gn_s, gn_r, val_s, val_r, w_s, w_r,
):
    rows, width = hid.shape
    fc = width // chunks
    rep, tp = lax.axis_index("rep"), lax.axis_index("tp")
    n_rep = lax.axis_size("rep")
    near = tp + 1 - 2 * lax.rem(tp, 2)
    far = lax.rem(tp + 2, 4)
    far_near = lax.rem(near + 2, 4)
    to_rep = lax.rem(rep + dist, n_rep)
    from_rep = lax.rem(rep + n_rep - dist, n_rep)
    near_dev, far_dev, to_dev, from_dev = (rep, near), (rep, far), (to_rep, tp), (from_rep, tp)

    def row_block(index):
        return pl.ds(pl.multiple_of(index * rows, rows), rows)

    barrier = pltpu.get_barrier_semaphore()
    for device in (near_dev, far_dev, to_dev, from_dev):
        pl.semaphore_signal(barrier, inc=1, device_id=device, device_id_type=MESH)
    loads = [
        pltpu.make_async_copy(num_hbm.at[0], num, load_sem.at[0]),
        pltpu.make_async_copy(hid_hbm, hid, load_sem.at[1]),
        pltpu.make_async_copy(cot_hbm.at[row_block(tp)], cot_own.at[pl.ds(0, rows)], load_sem.at[2]),
        pltpu.make_async_copy(cot_hbm.at[row_block(near)], cot_own.at[pl.ds(rows, rows)], load_sem.at[3]),
        pltpu.make_async_copy(m1_hbm.at[0], m1, load_sem.at[4]),
        pltpu.make_async_copy(m2_hbm.at[0], m2, load_sem.at[5]),
    ]
    for load in loads[:4]:
        load.start()
    weight = w_ref[0]
    w_send[...] = jnp.full(w_send.shape, weight, F32)
    part = [pl.ds(c * fc, fc) for c in range(chunks)]
    pl.semaphore_wait(barrier, 4)

    def remote(src, dst, send, recv, device):
        return pltpu.make_async_remote_copy(
            src_ref=src, dst_ref=dst, send_sem=send, recv_sem=recv, device_id=device, device_id_type=MESH
        )

    cot_copies = [
        remote(cot_hbm.at[row_block(far)], cot_far.at[pl.ds(0, rows)], cot_s.at[0], cot_r.at[0], far_dev),
        remote(cot_hbm.at[row_block(far_near)], cot_far.at[pl.ds(rows, rows)], cot_s.at[1], cot_r.at[1], far_dev),
    ]
    for copy in cot_copies:
        copy.start()
    nrm_copies = [
        remote(nrm.at[c, pl.ds(0, rows)], nrm.at[c, pl.ds(rows, rows)], nrm_s.at[c], nrm_r.at[c], near_dev)
        for c in range(chunks)
    ]
    deb_copies = [
        remote(deb_own.at[part[c]], deb_far.at[part[c]], deb_s.at[c], deb_r.at[c], far_dev) for c in range(chunks)
    ]
    g_copies = [
        remote(g_send.at[part[c]], g_far.at[part[c]], g_s.at[c], g_r.at[c], far_dev) for c in range(chunks)
    ]
    half_copies = [
        remote(half_send.at[part[c]], half_far.at[part[c]], half_s.at[c], half_r.at[c], to_dev)
        for c in range(chunks)
    ]
    gn_copies = [
        remote(gn_send.at[c], gn_near.at[c], gn_s.at[c], gn_r.at[c], near_dev) for c in range(chunks)
    ]
    val_copies = [
        remote(val_send.at[pl.ds(0, rows)], val_hbm.at[row_block(tp)], val_s.at[0], val_r.at[0], far_dev),
        remote(val_send.at[pl.ds(rows, rows)], val_hbm.at[row_block(near)], val_s.at[1], val_r.at[1], far_dev),
    ]
    w_copy = remote(w_send, w_far, w_s.at[0], w_r.at[0], to_dev)
    w_copy.start()

    def send_deb(c):
        deb_own[part[c], :] = (num[part[c], :] / jnp.full((1, 1), weight, F32)).astype(BF16)
        deb_copies[c].start()

    loads[0].wait()
    for c in range(EARLY):
        send_deb(c)
    loads[1].wait()
    step = 32

    @pl.loop(0, rows // step)
    def _(block):
        here = pl.ds(pl.multiple_of(block * step, step), step)
        x = hid[here, :].astype(F32)
        s = lax.rsqrt(jnp.mean(x * x, axis=1, keepdims=True) + 1e-06)
        scale[here, :] = s
        y = (x * s).astype(BF16)
        for c in range(chunks):
            nrm[c, here, :] = y[:, c * fc:(c + 1) * fc]

    for copy in nrm_copies:
        copy.start()

    for load in loads[4:]:
        load.start()
    loads[2].wait()
    loads[3].wait()
    for copy in cot_copies:
        copy.wait_recv()
    cot2 = jnp.concatenate([cot_own[...], cot_far[...]], axis=1)
    k = cot_own.shape[1]
    for c in range(chunks):
        nrm_copies[c].wait_recv()
        p = lax.dot_general(nrm[c], cot2, (((0,), (0,)), ((), ())), preferred_element_type=F32)
        g_send[part[c], :] = p[:, k:].astype(BF16)
        g_copies[c].start()
        g_own[part[c], :] = p[:, :k]
    for c in range(EARLY, chunks):
        send_deb(c)

    loads[4].wait()
    loads[5].wait()
    writes = []

    def write(src, dst):
        copy = pltpu.make_async_copy(src, dst, write_sem.at[len(writes)])
        copy.start()
        writes.append(copy)

    def moments(c):
        g_copies[c].wait_recv()
        here = part[c]
        grad = g_own[here, :] + g_far[here, :].astype(F32)
        first = 0.9 * m1[here, :] + 0.1 * grad
        second = 0.95 * m2[here, :] + 0.05 * grad * grad
        value = num[here, :]
        plain = value / jnp.full((1, 1), weight, F32)
        mine = value - 0.001 * (first / (jnp.sqrt(second) + 1e-08) + 0.1 * plain)
        half_send[here, :] = mine.astype(BF16)
        half_copies[c].start()
        half[here, :] = mine
        m1[here, :] = first
        m2[here, :] = second
        write(m1.at[here], m1o_hbm.at[0, here])
        write(m2.at[here], m2o_hbm.at[0, here])

    def swap_grad_normed(c, deb2):
        dims = (((1,), (1,)), ((), ()))
        both = jnp.concatenate([cot_own[pl.ds(rows, rows), :], cot_far[pl.ds(rows, rows), :]], axis=1)
        gn_send[c] = lax.dot_general(both, deb2, dims, preferred_element_type=F32).astype(BF16)
        gn_copies[c].start()
        both = jnp.concatenate([cot_own[pl.ds(0, rows), :], cot_far[pl.ds(0, rows), :]], axis=1)
        gn[c] = lax.dot_general(both, deb2, dims, preferred_element_type=F32)

    def forward(c):
        deb_copies[c].wait_recv()
        here = part[c]
        deb2 = jnp.concatenate([deb_own[here, :], deb_far[here, :]], axis=1)
        if c < chunks - 1:
            swap_grad_normed(c, deb2)
        product = jnp.dot(nrm[c], deb2, preferred_element_type=F32)
        if c:
            product = val_acc[...] + product
        if c < chunks - 1:
            val_acc[...] = product
        else:
            val_send[...] = product[:, k:].astype(BF16)
            for copy in val_copies:
                copy.start()
            swap_grad_normed(c, deb2)
            val_own[...] = product[:, :k].astype(BF16)
            write(val_own.at[pl.ds(0, rows)], val_hbm.at[row_block(tp)])
            write(val_own.at[pl.ds(rows, rows)], val_hbm.at[row_block(near)])

    def add_inner(c, inner):
        gn_copies[c].wait_recv()
        total = gn[c] + gn_near[c].astype(F32)
        gn[c] = total
        normal = hid[:, c * fc:(c + 1) * fc].astype(F32) * scale[...]
        return inner + jnp.sum(total * normal, axis=1, keepdims=True)

    def mix(c):
        half_copies[c].wait_recv()
        here = part[c]
        num[here, :] = 0.5 * (half[here, :] + half_far[here, :].astype(F32))
        write(num.at[here], numo_hbm.at[0, here])

    for c in range(chunks):
        moments(c)
    inner = jnp.zeros((rows, 1), F32)
    mixed = 0
    for c in range(chunks):
        forward(c)
        if c:
            inner = add_inner(c - 1, inner)
        ready = c if dist < 4 else c // 2
        while mixed < ready:
            mix(mixed)
            mixed += 1
    inner = add_inner(chunks - 1, inner) / width
    quarter = rows // 4
    for q in range(4):
        some = pl.ds(q * quarter, quarter)
        s = scale[some, :]
        mean = inner[q * quarter:(q + 1) * quarter]
        for c in range(chunks):
            normal = hid[some, c * fc:(c + 1) * fc].astype(F32) * s
            gh[some, c * fc:(c + 1) * fc] = (s * (gn[c, some, :] - normal * mean)).astype(BF16)
        write(gh.at[some], gh_hbm.at[some])
    for c in range(mixed, chunks):
        mix(c)
    w_copy.wait_recv()
    wo_ref[0] = 0.5 * (weight + jnp.max(w_far[...]))

    for copy in val_copies:
        copy.wait_recv()
    for group in (cot_copies, nrm_copies, deb_copies, g_copies, half_copies, gn_copies, val_copies, [w_copy]):
        for copy in group:
            copy.wait_send()
    for copy in writes:
        copy.wait()


def step_of(dist, level, chunks, operands):
    _, hidden, cotangent, numerator, moment_one, moment_two = operands
    rows, width = hidden.shape
    tokens, k = cotangent.shape
    fc = width // chunks
    any_space = pl.BlockSpec(memory_space=pl.ANY)
    smem = pl.BlockSpec(memory_space=pltpu.SMEM)
    dma = pltpu.SemaphoreType.DMA
    full32, full16 = pltpu.VMEM((width, k), F32), pltpu.VMEM((width, k), BF16)
    tok16 = pltpu.VMEM((2 * rows, k), BF16)
    small = pltpu.VMEM((8, 128), F32)
    shapes = [
        jax.ShapeDtypeStruct(numerator.shape, F32),
        jax.ShapeDtypeStruct((1,), F32),
        jax.ShapeDtypeStruct(moment_one.shape, F32),
        jax.ShapeDtypeStruct(moment_two.shape, F32),
        jax.ShapeDtypeStruct((tokens, k), BF16),
        jax.ShapeDtypeStruct((rows, width), BF16),
    ]
    scratch = [
        pltpu.VMEM((rows, width), BF16), full32, full32, full32, tok16, tok16,
        pltpu.VMEM((chunks, 2 * rows, fc), BF16), pltpu.VMEM((rows, 1), F32),
        full16, full16, full32, full16, full16, full32, full16, full16,
        pltpu.VMEM((chunks, rows, fc), F32), pltpu.VMEM((chunks, rows, fc), BF16),
        pltpu.VMEM((chunks, rows, fc), BF16), pltpu.VMEM((rows, width), BF16),
        pltpu.VMEM((2 * rows, 2 * k), F32), tok16, tok16, small, small,
        dma((6,)), dma((3 * chunks + 6,)),
        dma((2,)), dma((2,)),
    ] + [dma((chunks,))] * 10 + [dma((2,)), dma((2,)), dma((1,)), dma((1,))]
    return pl.pallas_call(
        functools.partial(kernel, dist, chunks),
        out_shape=shapes,
        in_specs=[smem] + [any_space] * 5,
        out_specs=[any_space, smem] + [any_space] * 4,
        scratch_shapes=scratch,
        compiler_params=pltpu.CompilerParams(
            collective_id=level, has_side_effects=True, vmem_limit_bytes=28 * 1024 * 1024
        ),
        cost_estimate=pl.CostEstimate(flops=12 * rows * width * 2 * k, bytes_accessed=12_000_000, transcendentals=0),
    )(*operands)


def place_kernel(held, count, weight_in, *refs):
    sources, weight_out, targets = refs[:count], refs[count], refs[count + 1:2 * count + 1]
    stages, (in_sem, out_sem) = refs[2 * count + 1:-2], refs[-2:]
    weight = pltpu.make_async_copy(weight_in, weight_out, out_sem.at[count])
    weight.start()
    arrivals = [
        pltpu.make_async_copy(source, stage, in_sem.at[index])
        for index, (source, stage) in enumerate(zip(sources[held:], stages))
    ]
    for arrival in arrivals:
        arrival.start()
    leaving = [
        pltpu.make_async_copy(source, target, out_sem.at[index])
        for index, (source, target) in enumerate(zip((*sources[:held], *stages), targets))
    ]
    for copy in leaving[:held]:
        copy.start()
    for arrival, copy in zip(arrivals, leaving[held:]):
        arrival.wait()
        copy.start()
    for copy in (*leaving, weight):
        copy.wait()


def place(weight, held, staged):
    arrays = [*held, *staged]
    any_space = pl.BlockSpec(memory_space=pl.ANY)
    in_vmem = pl.BlockSpec(memory_space=pltpu.VMEM)
    return pl.pallas_call(
        functools.partial(place_kernel, len(held), len(arrays)),
        out_shape=[jax.ShapeDtypeStruct(a.shape, a.dtype) for a in (weight, *arrays)],
        in_specs=[any_space] + [in_vmem] * len(held) + [any_space] * len(staged),
        out_specs=[any_space] * (1 + len(arrays)),
        scratch_shapes=[pltpu.VMEM(a.shape, a.dtype) for a in staged]
        + [pltpu.SemaphoreType.DMA((len(staged),)), pltpu.SemaphoreType.DMA((len(arrays) + 1,))],
        compiler_params=pltpu.CompilerParams(vmem_limit_bytes=16 * 1024 * 1024),
    )(weight, *arrays)


def local(hidden, cotangent, numerator, push_weight, moment_one, moment_two, gossip_round):
    operands = (push_weight, hidden, cotangent, numerator, moment_one, moment_two)
    branches = [
        (lambda items, level=level: tuple(step_of(2**level, level, CHUNKS, items))) for level in range(ROUNDS)
    ]
    numerator_out, weight_out, first, second, values, grad_hidden = lax.switch(gossip_round[0], branches, operands)
    weight_out, numerator_out, first, values, second, grad_hidden = place(
        weight_out, [numerator_out, first, values], [second, grad_hidden]
    )
    return numerator_out, weight_out, first, second, values, grad_hidden


def solution(mesh):
    placed = (
        P(("rep", "tp"), None),
        P("rep", "tp"),
        P("rep", None, "tp"),
        P("rep"),
        P("rep", None, "tp"),
        P("rep", None, "tp"),
        P(),
    )
    return jax.shard_map(
        local,
        mesh=mesh,
        in_specs=placed,
        out_specs=(
            P("rep", None, "tp"),
            P("rep"),
            P("rep", None, "tp"),
            P("rep", None, "tp"),
            P("rep", "tp"),
            P(("rep", "tp"), None),
        ),
        check_vma=False,
    )
```

```python
import functools

import jax
import jax.numpy as jnp
from jax import lax
from jax.experimental import pallas as pl
from jax.experimental.pallas import tpu as pltpu
from jax.sharding import PartitionSpec as P

MESH = pl.DeviceIdType.MESH
F32 = jnp.float32
BF16 = jnp.bfloat16
ROUNDS = 3
CHUNKS = 5
EARLY = 1


def kernel(
    dist, chunks,
    w_ref, hid_hbm, cot_hbm, num_hbm, m1_hbm, m2_hbm,
    numo_hbm, wo_ref, m1o_hbm, m2o_hbm, val_hbm, gh_hbm,
    hid, num, m1, m2, cot_own, cot_far, nrm, scale,
    deb_own, deb_far, g_own, g_send, g_far, half, half_send, half_far,
    gn, gn_send, gn_near, gh, val_acc, val_own, val_send, w_send, w_far,
    load_sem, write_sem,
    cot_s, cot_r, nrm_s, nrm_r, deb_s, deb_r, g_s, g_r, half_s, half_r, gn_s, gn_r, val_s, val_r, w_s, w_r,
):
    rows, width = hid.shape
    fc = width // chunks
    rep, tp = lax.axis_index("rep"), lax.axis_index("tp")
    n_rep = lax.axis_size("rep")
    near = tp + 1 - 2 * lax.rem(tp, 2)
    far = lax.rem(tp + 2, 4)
    far_near = lax.rem(near + 2, 4)
    to_rep = lax.rem(rep + dist, n_rep)
    from_rep = lax.rem(rep + n_rep - dist, n_rep)
    near_dev, far_dev, to_dev, from_dev = (rep, near), (rep, far), (to_rep, tp), (from_rep, tp)

    def row_block(index):
        return pl.ds(pl.multiple_of(index * rows, rows), rows)

    barrier = pltpu.get_barrier_semaphore()
    for device in (near_dev, far_dev, from_dev):
        pl.semaphore_signal(barrier, inc=1, device_id=device, device_id_type=MESH)
    loads = [
        pltpu.make_async_copy(num_hbm.at[0], num, load_sem.at[0]),
        pltpu.make_async_copy(hid_hbm, hid, load_sem.at[1]),
        pltpu.make_async_copy(cot_hbm.at[row_block(tp)], cot_own.at[pl.ds(0, rows)], load_sem.at[2]),
        pltpu.make_async_copy(cot_hbm.at[row_block(near)], cot_own.at[pl.ds(rows, rows)], load_sem.at[3]),
        pltpu.make_async_copy(m1_hbm.at[0], m1, load_sem.at[4]),
        pltpu.make_async_copy(m2_hbm.at[0], m2, load_sem.at[5]),
    ]
    for load in loads[:4]:
        load.start()
    weight = w_ref[0]
    w_send[...] = jnp.full(w_send.shape, weight, F32)
    part = [pl.ds(c * fc, fc) for c in range(chunks)]
    pl.semaphore_wait(barrier, 3)

    def remote(src, dst, send, recv, device):
        return pltpu.make_async_remote_copy(
            src_ref=src, dst_ref=dst, send_sem=send, recv_sem=recv, device_id=device, device_id_type=MESH
        )

    cot_copies = [
        remote(cot_hbm.at[row_block(far)], cot_far.at[pl.ds(0, rows)], cot_s.at[0], cot_r.at[0], far_dev),
        remote(cot_hbm.at[row_block(far_near)], cot_far.at[pl.ds(rows, rows)], cot_s.at[1], cot_r.at[1], far_dev),
    ]
    for copy in cot_copies:
        copy.start()
    nrm_copies = [
        remote(nrm.at[c, pl.ds(0, rows)], nrm.at[c, pl.ds(rows, rows)], nrm_s.at[c], nrm_r.at[c], near_dev)
        for c in range(chunks)
    ]
    deb_copies = [
        remote(deb_own.at[part[c]], deb_far.at[part[c]], deb_s.at[c], deb_r.at[c], far_dev) for c in range(chunks)
    ]
    g_copies = [
        remote(g_send.at[part[c]], g_far.at[part[c]], g_s.at[c], g_r.at[c], far_dev) for c in range(chunks)
    ]
    half_copies = [
        remote(half_send.at[part[c]], half_far.at[part[c]], half_s.at[c], half_r.at[c], to_dev)
        for c in range(chunks)
    ]
    gn_copies = [
        remote(gn_send.at[c], gn_near.at[c], gn_s.at[c], gn_r.at[c], near_dev) for c in range(chunks)
    ]
    val_copies = [
        remote(val_send.at[pl.ds(0, rows)], val_hbm.at[row_block(tp)], val_s.at[0], val_r.at[0], far_dev),
        remote(val_send.at[pl.ds(rows, rows)], val_hbm.at[row_block(near)], val_s.at[1], val_r.at[1], far_dev),
    ]
    w_copy = remote(w_send, w_far, w_s.at[0], w_r.at[0], to_dev)
    w_copy.start()

    def send_deb(c):
        deb_own[part[c], :] = (num[part[c], :] / jnp.full((1, 1), weight, F32)).astype(BF16)
        deb_copies[c].start()

    loads[0].wait()
    for c in range(EARLY):
        send_deb(c)
    loads[1].wait()
    step = 32

    @pl.loop(0, rows // step)
    def _(block):
        here = pl.ds(pl.multiple_of(block * step, step), step)
        x = hid[here, :].astype(F32)
        s = lax.rsqrt(jnp.mean(x * x, axis=1, keepdims=True) + 1e-06)
        scale[here, :] = s
        y = (x * s).astype(BF16)
        for c in range(chunks):
            nrm[c, here, :] = y[:, c * fc:(c + 1) * fc]

    for copy in nrm_copies:
        copy.start()

    for load in loads[4:]:
        load.start()
    loads[2].wait()
    loads[3].wait()
    for copy in cot_copies:
        copy.wait_recv()
    cot2 = jnp.concatenate([cot_own[...], cot_far[...]], axis=1)
    k = cot_own.shape[1]
    for c in range(chunks):
        nrm_copies[c].wait_recv()
        p = lax.dot_general(nrm[c], cot2, (((0,), (0,)), ((), ())), preferred_element_type=F32)
        g_send[part[c], :] = p[:, k:].astype(BF16)
        g_copies[c].start()
        g_own[part[c], :] = p[:, :k]
    for c in range(EARLY, chunks):
        send_deb(c)

    loads[4].wait()
    loads[5].wait()
    writes = []

    def write(src, dst):
        copy = pltpu.make_async_copy(src, dst, write_sem.at[len(writes)])
        copy.start()
        writes.append(copy)

    def moments(c):
        g_copies[c].wait_recv()
        here = part[c]
        grad = g_own[here, :] + g_far[here, :].astype(F32)
        first = 0.9 * m1[here, :] + 0.1 * grad
        second = 0.95 * m2[here, :] + 0.05 * grad * grad
        value = num[here, :]
        plain = value / jnp.full((1, 1), weight, F32)
        mine = value - 0.001 * (first / (jnp.sqrt(second) + 1e-08) + 0.1 * plain)
        half_send[here, :] = mine.astype(BF16)
        half_copies[c].start()
        half[here, :] = mine
        m1[here, :] = first
        m2[here, :] = second
        write(m1.at[here], m1o_hbm.at[0, here])
        write(m2.at[here], m2o_hbm.at[0, here])

    def swap_grad_normed(c, deb2):
        dims = (((1,), (1,)), ((), ()))
        both = jnp.concatenate([cot_own[pl.ds(rows, rows), :], cot_far[pl.ds(rows, rows), :]], axis=1)
        gn_send[c] = lax.dot_general(both, deb2, dims, preferred_element_type=F32).astype(BF16)
        gn_copies[c].start()
        both = jnp.concatenate([cot_own[pl.ds(0, rows), :], cot_far[pl.ds(0, rows), :]], axis=1)
        gn[c] = lax.dot_general(both, deb2, dims, preferred_element_type=F32)

    def forward(c):
        deb_copies[c].wait_recv()
        here = part[c]
        deb2 = jnp.concatenate([deb_own[here, :], deb_far[here, :]], axis=1)
        if c < chunks - 1:
            swap_grad_normed(c, deb2)
        product = jnp.dot(nrm[c], deb2, preferred_element_type=F32)
        if c:
            product = val_acc[...] + product
        if c < chunks - 1:
            val_acc[...] = product
        else:
            val_send[...] = product[:, k:].astype(BF16)
            for copy in val_copies:
                copy.start()
            swap_grad_normed(c, deb2)
            val_own[...] = product[:, :k].astype(BF16)
            write(val_own.at[pl.ds(0, rows)], val_hbm.at[row_block(tp)])
            write(val_own.at[pl.ds(rows, rows)], val_hbm.at[row_block(near)])

    def add_inner(c, inner):
        gn_copies[c].wait_recv()
        total = gn[c] + gn_near[c].astype(F32)
        gn[c] = total
        normal = hid[:, c * fc:(c + 1) * fc].astype(F32) * scale[...]
        return inner + jnp.sum(total * normal, axis=1, keepdims=True)

    def mix(c):
        half_copies[c].wait_recv()
        here = part[c]
        num[here, :] = 0.5 * (half[here, :] + half_far[here, :].astype(F32))
        write(num.at[here], numo_hbm.at[0, here])

    for c in range(chunks):
        moments(c)
    inner = jnp.zeros((rows, 1), F32)
    mixed = 0
    for c in range(chunks):
        forward(c)
        if c:
            inner = add_inner(c - 1, inner)
        ready = c if dist < 4 else c // 2
        while mixed < ready:
            mix(mixed)
            mixed += 1
    inner = add_inner(chunks - 1, inner) / width
    quarter = rows // 4
    for q in range(4):
        some = pl.ds(q * quarter, quarter)
        s = scale[some, :]
        mean = inner[q * quarter:(q + 1) * quarter]
        for c in range(chunks):
            normal = hid[some, c * fc:(c + 1) * fc].astype(F32) * s
            gh[some, c * fc:(c + 1) * fc] = (s * (gn[c, some, :] - normal * mean)).astype(BF16)
        write(gh.at[some], gh_hbm.at[some])
    for c in range(mixed, chunks):
        mix(c)
    w_copy.wait_recv()
    wo_ref[0] = 0.5 * (weight + jnp.max(w_far[...]))

    for copy in val_copies:
        copy.wait_recv()
    for group in (cot_copies, nrm_copies, deb_copies, g_copies, half_copies, gn_copies, val_copies, [w_copy]):
        for copy in group:
            copy.wait_send()
    for copy in writes:
        copy.wait()


def step_of(dist, level, chunks, operands):
    _, hidden, cotangent, numerator, moment_one, moment_two = operands
    rows, width = hidden.shape
    tokens, k = cotangent.shape
    fc = width // chunks
    any_space = pl.BlockSpec(memory_space=pl.ANY)
    smem = pl.BlockSpec(memory_space=pltpu.SMEM)
    dma = pltpu.SemaphoreType.DMA
    full32, full16 = pltpu.VMEM((width, k), F32), pltpu.VMEM((width, k), BF16)
    tok16 = pltpu.VMEM((2 * rows, k), BF16)
    small = pltpu.VMEM((8, 128), F32)
    shapes = [
        jax.ShapeDtypeStruct(numerator.shape, F32),
        jax.ShapeDtypeStruct((1,), F32),
        jax.ShapeDtypeStruct(moment_one.shape, F32),
        jax.ShapeDtypeStruct(moment_two.shape, F32),
        jax.ShapeDtypeStruct((tokens, k), BF16),
        jax.ShapeDtypeStruct((rows, width), BF16),
    ]
    scratch = [
        pltpu.VMEM((rows, width), BF16), full32, full32, full32, tok16, tok16,
        pltpu.VMEM((chunks, 2 * rows, fc), BF16), pltpu.VMEM((rows, 1), F32),
        full16, full16, full32, full16, full16, full32, full16, full16,
        pltpu.VMEM((chunks, rows, fc), F32), pltpu.VMEM((chunks, rows, fc), BF16),
        pltpu.VMEM((chunks, rows, fc), BF16), pltpu.VMEM((rows, width), BF16),
        pltpu.VMEM((2 * rows, 2 * k), F32), tok16, tok16, small, small,
        dma((6,)), dma((3 * chunks + 6,)),
        dma((2,)), dma((2,)),
    ] + [dma((chunks,))] * 10 + [dma((2,)), dma((2,)), dma((1,)), dma((1,))]
    return pl.pallas_call(
        functools.partial(kernel, dist, chunks),
        out_shape=shapes,
        in_specs=[smem] + [any_space] * 5,
        out_specs=[any_space, smem] + [any_space] * 4,
        scratch_shapes=scratch,
        compiler_params=pltpu.CompilerParams(
            collective_id=level, has_side_effects=True, vmem_limit_bytes=28 * 1024 * 1024
        ),
        cost_estimate=pl.CostEstimate(flops=12 * rows * width * 2 * k, bytes_accessed=12_000_000, transcendentals=0),
    )(*operands)


def place_kernel(held, count, weight_in, *refs):
    sources, weight_out, targets = refs[:count], refs[count], refs[count + 1:2 * count + 1]
    stages, (in_sem, out_sem) = refs[2 * count + 1:-2], refs[-2:]
    weight = pltpu.make_async_copy(weight_in, weight_out, out_sem.at[count])
    weight.start()
    arrivals = [
        pltpu.make_async_copy(source, stage, in_sem.at[index])
        for index, (source, stage) in enumerate(zip(sources[held:], stages))
    ]
    for arrival in arrivals:
        arrival.start()
    leaving = [
        pltpu.make_async_copy(source, target, out_sem.at[index])
        for index, (source, target) in enumerate(zip((*sources[:held], *stages), targets))
    ]
    for copy in leaving[:held]:
        copy.start()
    for arrival, copy in zip(arrivals, leaving[held:]):
        arrival.wait()
        copy.start()
    for copy in (*leaving, weight):
        copy.wait()


def place(weight, held, staged):
    arrays = [*held, *staged]
    any_space = pl.BlockSpec(memory_space=pl.ANY)
    in_vmem = pl.BlockSpec(memory_space=pltpu.VMEM)
    return pl.pallas_call(
        functools.partial(place_kernel, len(held), len(arrays)),
        out_shape=[jax.ShapeDtypeStruct(a.shape, a.dtype) for a in (weight, *arrays)],
        in_specs=[any_space] + [in_vmem] * len(held) + [any_space] * len(staged),
        out_specs=[any_space] * (1 + len(arrays)),
        scratch_shapes=[pltpu.VMEM(a.shape, a.dtype) for a in staged]
        + [pltpu.SemaphoreType.DMA((len(staged),)), pltpu.SemaphoreType.DMA((len(arrays) + 1,))],
        compiler_params=pltpu.CompilerParams(vmem_limit_bytes=16 * 1024 * 1024),
    )(weight, *arrays)


def local(hidden, cotangent, numerator, push_weight, moment_one, moment_two, gossip_round):
    operands = (push_weight, hidden, cotangent, numerator, moment_one, moment_two)
    branches = [
        (lambda items, level=level: tuple(step_of(2**level, level, CHUNKS, items))) for level in range(ROUNDS)
    ]
    numerator_out, weight_out, first, second, values, grad_hidden = lax.switch(gossip_round[0], branches, operands)
    weight_out, numerator_out, first, values, second, grad_hidden = place(
        weight_out, [numerator_out, first, values], [second, grad_hidden]
    )
    return numerator_out, weight_out, first, second, values, grad_hidden


def solution(mesh):
    placed = (
        P(("rep", "tp"), None),
        P("rep", "tp"),
        P("rep", None, "tp"),
        P("rep"),
        P("rep", None, "tp"),
        P("rep", None, "tp"),
        P(),
    )
    return jax.shard_map(
        local,
        mesh=mesh,
        in_specs=placed,
        out_specs=(
            P("rep", None, "tp"),
            P("rep"),
            P("rep", None, "tp"),
            P("rep", None, "tp"),
            P("rep", "tp"),
            P(("rep", "tp"), None),
        ),
        check_vma=False,
    )
```
